256 devices in a mesh: seq: 8 (over y_hi, x), row: 8 (over z), col: 4 (over y_lo, core).
Axes of the slice: x: 4, y: 4 (y_hi: 2, y_lo: 2; y = y_hi * 2 + y_lo), z: 8, core: 2. Of those that a mesh axis runs over, the one named last changes fastest.
Arguments:
- alignment: int32 [32768, 256], P('seq'), may hold values from 0 to 20, as said below
- cluster_sizes: int32 [32768], P('seq'), may hold values from 1 to 32, as said below
- block_inverse: float32 [128, 128], replicated, may hold values from -12 to 12
Outputs:
- couplings: float32 [5120, 5120], P(('seq', 'row'), 'col')
The draws below stay inside these ranges and needn't reach their ends.
Inputs may be any that keep to these rules, and one draw needn't show every extreme that they name: `alignment`: the value 20 marks a gap. `cluster_sizes`: every cluster size is a power of two.
All inputs are finite; a program needn't handle non-finite values.
Results may differ from the reference program's by a relative error of at most 0.0003.
Values sent between devices are 32-bit elements; how exact they have to be, the bound alone decides.
A program may use at most 64 MiB of HBM per device.

```python
import jax
import jax.numpy as jnp
from jax import lax

Q = 20
POS = 256
PANEL = 128
SEQS = 32768


def draw_alignment(key, part):
    keys = jax.random.split(key, 5)
    groups = POS // 4
    latent = jax.random.randint(keys[0], (SEQS, groups), 0, Q + 1)
    offsets = jax.random.randint(keys[1], (1, POS), 0, Q + 1)
    noise_rate = jax.random.randint(keys[2], (1, POS), 1, 5)
    noise_pick = jax.random.randint(keys[3], (SEQS, POS), 0, 8)
    noise_state = jax.random.randint(keys[4], (SEQS, POS), 0, Q + 1)
    coupled = (jnp.tile(latent, (1, 4)) + offsets) % (Q + 1)
    return jnp.where(noise_pick < noise_rate, noise_state, coupled).astype(jnp.int32)


def draw_cluster_sizes(key, part):
    index = jnp.arange(SEQS, dtype=jnp.int32)
    ceiling = 2 + 4 * (SEQS - 1 - index) // max(SEQS - 1, 1)
    raw_bits = jax.random.randint(key, (SEQS,), 0, 1 << 20)
    exponent = raw_bits % ceiling
    exponent = jnp.where(index == 0, 5, exponent)
    exponent = jnp.where(index == SEQS - 1, 0, exponent)
    sizes = jnp.left_shift(jnp.ones((SEQS,), jnp.int32), exponent.astype(jnp.int32))
    return sizes.astype(jnp.int32)


def gaussian(stream_key, shape, spread, bound, held_as=jnp.bfloat16):
    values = spread * jax.random.normal(stream_key, shape, jnp.float32)
    return jnp.clip(values, min=-bound, max=bound).astype(held_as)


def setup_inputs(seed: int = 0) -> dict:
    arg_keys = jax.random.split(jax.random.key(seed), 4)
    alignment = draw_alignment(jax.random.fold_in(arg_keys[3], 71), 0)
    cluster_sizes = draw_cluster_sizes(jax.random.fold_in(arg_keys[3], 71), 0)
    block_inverse = gaussian(arg_keys[2], (PANEL, PANEL), 2.0, 12.0, jnp.float32)
    return dict(alignment=alignment, cluster_sizes=cluster_sizes, block_inverse=block_inverse)


PSEUDOCOUNT = 0.5


def one_hot_states(states, span_width):
    levels = lax.broadcasted_iota(jnp.int32, (1, 1, Q), 2)
    matches = (states[:, :, None] == levels).astype(jnp.bfloat16)
    return matches.reshape(states.shape[0], states.shape[1] * Q)[:, :span_width]


def covariance_block(pair_block, row_margin, col_margin, weight_total, row_start, col_start):
    row_freq = (1.0 - PSEUDOCOUNT) * row_margin / weight_total + PSEUDOCOUNT / Q
    col_freq = (1.0 - PSEUDOCOUNT) * col_margin / weight_total + PSEUDOCOUNT / Q
    shape_rc = pair_block.shape
    row_ids = row_start + lax.broadcasted_iota(jnp.int32, shape_rc, 0)
    col_ids = col_start + lax.broadcasted_iota(jnp.int32, shape_rc, 1)
    same_pos = (row_ids // Q) == (col_ids // Q)
    prior = jnp.where(same_pos, jnp.where(row_ids == col_ids, PSEUDOCOUNT / Q, 0.0), PSEUDOCOUNT / (Q * Q))
    joint = (1.0 - PSEUDOCOUNT) * pair_block / weight_total + prior
    return joint - row_freq[:, None] * col_freq[None, :]


def reference(alignment, cluster_sizes, block_inverse):
    features = POS * Q
    seq_weight = (1.0 / cluster_sizes.astype(jnp.float32)).astype(jnp.bfloat16)
    weight_total = jnp.sum(seq_weight.astype(jnp.float32))
    block_rows = min(SEQS, 4096)
    count_blocks = SEQS // block_rows
    states_blocks = alignment.reshape(count_blocks, block_rows, POS)
    weight_blocks = seq_weight.reshape(count_blocks, block_rows)

    def add_block(running, block_item):
        pair_total, margin_total = running
        states_block, weight_block = block_item
        onehot = one_hot_states(states_block, features)
        weighted = onehot * weight_block[:, None]
        pair_total = pair_total + lax.dot_general(weighted, onehot, (((0,), (0,)), ((), ())), preferred_element_type=jnp.float32)
        margin_total = margin_total + jnp.dot(weight_block, onehot, preferred_element_type=jnp.float32)
        return (pair_total, margin_total), None

    initial = (jnp.zeros((features, features), jnp.float32), jnp.zeros((features,), jnp.float32))
    (pair_total, margin_total), unused = lax.scan(add_block, initial, (states_blocks, weight_blocks))
    cov = covariance_block(pair_total, margin_total, margin_total, weight_total, 0, 0)
    panel = cov[:, :PANEL]
    sym_inverse = 0.5 * (block_inverse + block_inverse.T)
    left_factor = jnp.dot(panel, sym_inverse, precision=lax.Precision.HIGHEST)
    update = lax.dot_general(left_factor, panel, (((1,), (1,)), ((), ())), precision=lax.Precision.HIGHEST)
    return -Q * (cov - update)
```

```python
import jax
import jax.numpy as jnp
from jax import lax
from jax.experimental import pallas as pl
from jax.experimental.pallas import tpu as pltpu
from jax.sharding import PartitionSpec as P

Q = 20
POS = 256
PANEL = 128
SEQS_LOCAL = 4096
ROWS = 80
COLS = 1280
CHUNK = 256
CHUNKS = COLS // CHUNK
MAIN = 640
LEFT = 672
LOAD = 512
LANES = 128
HOT = jnp.float8_e4m3fn
F32 = jnp.float32
MESH = pl.DeviceIdType.MESH
X_FIRST = (True, False, True, False, True)
N_COPIES = 80
HIGHEST = lax.Precision.HIGHEST
CONTRACT_LAST = (((1,), (1,)), ((), ()))


def position_of(feature):
    return (feature * 3277) >> 16


def hot_rows(state_row, value):
    lanes = LANES
    row = lax.broadcasted_iota(jnp.int32, (8, lanes), 0).astype(F32)
    parts = []
    for tile in range(Q):
        low = 8 * tile
        first, last = low // Q, (low + 7) // Q
        base = float(low - Q * first)
        states = jnp.broadcast_to(state_row(first), (8, lanes))
        level = row + base
        if last != first:
            cut = float(Q * last - low)
            before = row < cut
            states = jnp.where(before, states, jnp.broadcast_to(state_row(last), (8, lanes)))
            level = jnp.where(before, level, row - cut)
        parts.append(jnp.where(states == level, value, 0.0))
    return jnp.concatenate(parts, 0)


def kernel(
    align_hbm, sizes_ref, inverse_ref, out_ref,
    align, states, left, right, pairs, xr, yr, yr4, final, eu, er, es, eg, zg, mc, pr, panel_t,
    load_sem, send_sem, recv_sem,
):
    s = lax.axis_index("seq")
    r = lax.axis_index("row")
    c = lax.axis_index("col")
    yh, x = s // 4, s % 4
    x_next, x_far, x_prev = (x + 1) % 4, (x + 2) % 4, (x + 3) % 4
    loads = []
    for i in range(SEQS_LOCAL // LOAD):
        rows = pl.ds(i * LOAD, LOAD)
        copy = pltpu.make_async_copy(align_hbm.at[rows, :], align.at[rows, :], load_sem.at[i])
        copy.start()
        loads.append(copy)

    def seq_of(to_yh, to_x):
        return to_yh * 4 + to_x

    def at_seq(dx, dy):
        return (seq_of((yh + dy) % 2, (x + dx) % 4), r, c)

    barrier = pltpu.get_barrier_semaphore()
    peers = [at_seq(dx, dy) for dx in range(4) for dy in range(2) if dx or dy]
    peers += [(s, (r + dz) % 8, c) for dz in range(1, 8)]
    peers += [(s, r, (c + dc) % 4) for dc in range(1, 4)]
    for peer in peers:
        pl.semaphore_signal(barrier, inc=1, device_id=peer, device_id_type=MESH)

    used = []
    sends = []

    def push(src, dst, device):
        index = len(used)
        used.append(index)
        copy = pltpu.make_async_remote_copy(
            src_ref=src, dst_ref=dst, send_sem=send_sem.at[index], recv_sem=recv_sem.at[index],
            device_id=device, device_id_type=MESH,
        )
        copy.start()
        sends.append(copy)
        return copy

    row_id = lax.broadcasted_iota(jnp.int32, (112, POS), 0)
    pos_id = lax.broadcasted_iota(jnp.int32, (112, POS), 1)
    wanted = jnp.where(
        row_id < 32,
        (row_id >> 2) * 32 + r * 4 + (row_id & 3),
        jnp.where(row_id < 96, c * 64 + row_id - 32, position_of(r * 16 + row_id - 96)),
    )
    pick = (pos_id == wanted).astype(F32).astype(jnp.bfloat16)
    for i in range(SEQS_LOCAL // LOAD):
        loads[i].wait()
        block = align[pl.ds(i * LOAD, LOAD), :].astype(F32).astype(jnp.bfloat16)
        states[:, pl.ds(i * LOAD, LOAD)] = lax.dot_general(
            pick, block, CONTRACT_LAST, preferred_element_type=F32
        )

    feature = r * 16 + lax.broadcasted_iota(jnp.int32, (16, LANES), 0)
    panel_level = (feature - position_of(feature) * Q).astype(F32)
    first_row = lax.broadcasted_iota(jnp.int32, (16, LANES), 0) == 0

    @pl.loop(0, SEQS_LOCAL // LANES)
    def _(i):
        lanes = pl.ds(pl.multiple_of(i * LANES, LANES), LANES)
        weight = 1.0 / sizes_ref[pl.ds(i, 1), :].astype(F32)
        weight8 = jnp.broadcast_to(weight, (8, LANES))
        weight16 = jnp.broadcast_to(weight, (16, LANES))
        for b in range(4):
            left[pl.ds(160 * b, 160), lanes] = hot_rows(
                lambda p: states[pl.ds(b * 8 + p, 1), lanes], weight8
            ).astype(HOT)
        panel_hot = jnp.where(states[pl.ds(96, 16), lanes] == panel_level, weight16, 0.0)
        weight_row = jnp.where(first_row, weight16, 0.0)
        left[pl.ds(MAIN, 32), lanes] = jnp.concatenate([panel_hot, weight_row], 0).astype(HOT)
        for b in range(8):
            right[pl.ds(160 * b, 160), lanes] = hot_rows(
                lambda p: states[pl.ds(32 + b * 8 + p, 1), lanes], 1.0
            ).astype(HOT)

    def multiply(j):
        pairs[j] = lax.dot_general(
            left[...], right[pl.ds(j * CHUNK, CHUNK), :], CONTRACT_LAST, preferred_element_type=F32
        )

    def block(j, to_yh, to_x, low=0, size=ROWS):
        start = pl.multiple_of(seq_of(to_yh, to_x) * ROWS + low, 8)
        return pairs.at[j, pl.ds(start, size), :]

    copies = {}

    def stage_one(j):
        if X_FIRST[j]:
            k = X_FIRST[:j].count(True)
            copies[j] = [
                push(block(j, 0, x_far), xr.at[k, 0], at_seq(1, 0)),
                push(block(j, 1, x_far), xr.at[k, 1], at_seq(3, 0)),
                push(block(j, 1, x_next), xr.at[k, 2], at_seq(1, 0)),
                push(block(j, 0, x_prev), xr.at[k, 3], at_seq(3, 0)),
            ]
        else:
            k = X_FIRST[:j].count(False)
            copies[j] = [
                push(block(j, 1 - yh, to_x), yr4.at[k, i], at_seq(0, 1))
                for i, to_x in enumerate((x_far, x_next, x_prev, x))
            ]

    def stage_two(j):
        done = copies[j]
        if X_FIRST[j]:
            k = X_FIRST[:j].count(True)
            done[0].wait_recv()
            target = block(j, 0, x_next)
            target[...] += xr[k, 0]
            done.append(push(target, xr.at[k, 4], at_seq(1, 0)))
            done[1].wait_recv()
            target = block(j, 1, x_prev)
            target[...] += xr[k, 1]
            done.append(push(target, xr.at[k, 5], at_seq(3, 0)))
        else:
            k = X_FIRST[:j].count(False)
            done[0].wait_recv()
            yr4[k, 0] += block(j, yh, x_far)[...]
            done.append(push(yr4.at[k, 0, pl.ds(0, 40), :], yr.at[k, 0], at_seq(1, 0)))
            done.append(push(yr4.at[k, 0, pl.ds(40, 40), :], yr.at[k, 1], at_seq(3, 0)))
            done[1].wait_recv()
            yr4[k, 1] += block(j, yh, x_next)[...]
            done.append(push(yr4.at[k, 1, pl.ds(40, 40), :], yr.at[k, 2], at_seq(1, 0)))
            done[2].wait_recv()
            yr4[k, 2] += block(j, yh, x_prev)[...]
            done.append(push(yr4.at[k, 2, pl.ds(0, 40), :], yr.at[k, 3], at_seq(3, 0)))

    def stage_three(j):
        done = copies[j]
        if X_FIRST[j]:
            k = X_FIRST[:j].count(True)
            for i in range(2, 6):
                done[i].wait_recv()
            mine = block(j, 0, x)
            mine[...] += xr[k, 4] + xr[k, 3]
            mine = block(j, 1, x)
            mine[...] += xr[k, 2] + xr[k, 5]
            done.append(push(block(j, 1 - yh, x), xr.at[k, 6], at_seq(0, 1)))
        else:
            k = X_FIRST[:j].count(False)
            done[4].wait_recv()
            yr4[k, 1, pl.ds(0, 40), :] += yr[k, 0]
            done.append(push(yr4.at[k, 1, pl.ds(0, 40), :], yr.at[k, 4], at_seq(1, 0)))
            done[5].wait_recv()
            yr4[k, 2, pl.ds(40, 40), :] += yr[k, 1]
            done.append(push(yr4.at[k, 2, pl.ds(40, 40), :], yr.at[k, 5], at_seq(3, 0)))

    def finish(j):
        done = copies[j]
        if X_FIRST[j]:
            k = X_FIRST[:j].count(True)
            done[6].wait_recv()
            final[j] = block(j, yh, x)[...] + xr[k, 6]
        else:
            k = X_FIRST[:j].count(False)
            for i in (3, 6, 7, 8, 9):
                done[i].wait_recv()
            own = block(j, yh, x)
            final[j, pl.ds(0, 40), :] = (
                own[pl.ds(0, 40), :] + yr4[k, 3, pl.ds(0, 40), :] + yr[k, 4] + yr[k, 3]
            )
            final[j, pl.ds(40, 40), :] = (
                own[pl.ds(40, 40), :] + yr4[k, 3, pl.ds(40, 40), :] + yr[k, 2] + yr[k, 5]
            )

    def lane_tile(tile):
        return tile // 2, pl.ds((tile % 2) * LANES, LANES)

    multiply(0)
    pl.semaphore_wait(barrier, len(peers))
    stage_one(0)
    multiply(1)
    stage_one(1)
    multiply(2)
    stage_one(2)
    stage_two(0)
    multiply(3)
    stage_one(3)
    stage_two(1)
    multiply(4)

    weight_sum = jnp.sum(
        jnp.sum(1.0 / sizes_ref[...].astype(F32), axis=0, keepdims=True), axis=1, keepdims=True
    )
    for u in range(4):
        g, h = u // 2, u % 2
        for t in range(5):
            j, lanes = lane_tile(h * 5 + t)
            eu[u, pl.ds(8 * t, 8), :] = pairs[j, pl.ds(MAIN + 8 * g, 8), lanes]
        for tile in range(10):
            j, lanes = lane_tile(tile)
            eu[u, pl.ds(40 + tile, 1), :] = pairs[j, pl.ds(MAIN + 16, 1), lanes]
        eu[u, pl.ds(50, 6), :] = jnp.broadcast_to(weight_sum, (6, LANES))
    panel_sums = []
    for dx in range(4):
        for dy in range(2):
            if dx or dy:
                panel_sums.append(
                    push(eu.at[(x + dx) % 4], er.at[dx * 2 + dy - 1], at_seq(dx, dy))
                )
    stage_one(4)
    stage_two(2)
    stage_three(0)
    for copy in panel_sums:
        copy.wait_recv()
    total = eu[x]
    for i in range(7):
        total = total + er[i]
    eg[x] = total[0:40]
    mc[c] = total[40:56]
    es[...] = total
    panel_gathers = [
        push(es.at[pl.ds(0, 40), :], eg.at[x], at_seq(dx, 0)) for dx in range(1, 4)
    ]
    margin_gathers = [
        push(es.at[pl.ds(40, 16), :], mc.at[c], (s, r, (c + dc) % 4)) for dc in range(1, 4)
    ]
    stage_two(3)
    stage_three(1)
    for copy in panel_gathers:
        copy.wait_recv()
    zg[r] = eg[...]
    z_gathers = [push(eg, zg.at[r], (s, (r + dz) % 8, c)) for dz in range(1, 8)]
    finish(0)
    row_index = [len(used) + i for i in range(3)]
    used.extend(row_index)

    def row_copy(i):
        return pltpu.make_async_remote_copy(
            src_ref=final.at[0, :, pl.ds(0, PANEL)], dst_ref=pr,
            send_sem=send_sem.at[row_index[i]], recv_sem=recv_sem.at[row_index[0]],
            device_id=(s, r, (c + 1 + i) % 4), device_id_type=MESH,
        )

    @pl.when(c == 0)
    def _():
        for i in range(3):
            row_copy(i).start()
        pr[...] = final[0, :, pl.ds(0, PANEL)]

    stage_two(4)
    stage_three(2)
    stage_three(3)
    finish(1)
    stage_three(4)
    finish(2)
    finish(3)

    @pl.when(c != 0)
    def _():
        row_copy(0).wait_recv()

    for copy in margin_gathers:
        copy.wait_recv()
    half = 0.5 / mc[c, pl.ds(10, 1), :]
    floor = 0.5 / Q
    half_cols = jnp.concatenate([half] * 10, 1)
    col_freq = (
        jnp.concatenate([mc[c, pl.ds(i, 1), :] for i in range(10)], 1) * half_cols + floor
    )
    panel_freq = mc[0, pl.ds(0, 1), :] * half + floor
    row_low = (s * 8 + r) * ROWS
    local = (s % 2) * MAIN + r * ROWS + lax.broadcasted_iota(jnp.int32, (ROWS, LANES), 0)
    lane = lax.broadcasted_iota(jnp.int32, (ROWS, LANES), 1)
    found = jnp.zeros((ROWS, LANES), F32)
    for i in range(10):
        found += jnp.where(
            local == lane + i * LANES, jnp.broadcast_to(mc[s // 2, pl.ds(i, 1), :] * half, (ROWS, LANES)), 0.0
        )
    row_freq = jnp.sum(found, axis=1, keepdims=True) + floor
    eye = lax.broadcasted_iota(jnp.int32, (PANEL, PANEL), 0) == lax.broadcasted_iota(
        jnp.int32, (PANEL, PANEL), 1
    )
    panel_freq_column = jnp.sum(
        jnp.where(eye, jnp.broadcast_to(panel_freq, (PANEL, PANEL)), 0.0), axis=1, keepdims=True
    )

    def covariance(sums, scale, freq_rows, freq_cols, first, col_first):
        shape = sums.shape
        row = first + lax.broadcasted_iota(jnp.int32, shape, 0)
        col = col_first + lax.broadcasted_iota(jnp.int32, shape, 1)
        prior = jnp.where(
            position_of(row) == position_of(col),
            jnp.where(row == col, 0.5 / Q, 0.0),
            0.5 / (Q * Q),
        )
        return sums * scale + prior - freq_rows * freq_cols

    panel_rows = covariance(pr[...], half, row_freq, panel_freq, row_low, 0)
    symmetric = 0.5 * (inverse_ref[...] + inverse_ref[...].T)
    factor = jnp.dot(panel_rows, symmetric, precision=HIGHEST, preferred_element_type=F32)
    for copy in z_gathers:
        copy.wait_recv()
    for tile in range(10):
        h, t = tile // 5, tile % 5
        for k in range(16):
            panel_t[tile // 2, pl.ds(8 * k, 8), pl.ds((tile % 2) * LANES, LANES)] = zg[
                k // 2, (k % 2) * 2 + h, pl.ds(8 * t, 8), :
            ]
    for j in range(CHUNKS):
        if j == CHUNKS - 1:
            finish(4)
        columns = pl.ds(j * CHUNK, CHUNK)
        scale = half_cols[:, j * CHUNK:(j + 1) * CHUNK]
        freq = col_freq[:, j * CHUNK:(j + 1) * CHUNK]
        col_low = c * COLS + j * CHUNK
        panel_cols = covariance(panel_t[j], scale, panel_freq_column, freq, 0, col_low)
        update = jnp.dot(factor, panel_cols, precision=HIGHEST, preferred_element_type=F32)
        cov = covariance(final[j], scale, row_freq, freq, row_low, col_low)
        out_ref[:, columns] = -float(Q) * (cov - update)

    for copy in sends:
        copy.wait_send()

    @pl.when(c == 0)
    def _():
        for i in range(3):
            row_copy(i).wait_send()

    assert len(used) <= N_COPIES


def shards(alignment, cluster_sizes, block_inverse):
    x_chunks = X_FIRST.count(True)
    y_chunks = X_FIRST.count(False)
    vmem = pl.BlockSpec(memory_space=pltpu.VMEM)
    return pl.pallas_call(
        kernel,
        out_shape=jax.ShapeDtypeStruct((ROWS, COLS), F32),
        in_specs=[pl.BlockSpec(memory_space=pl.ANY), vmem, vmem],
        out_specs=vmem,
        scratch_shapes=[
            pltpu.VMEM((SEQS_LOCAL, POS), jnp.int32),
            pltpu.VMEM((112, SEQS_LOCAL), F32),
            pltpu.VMEM((LEFT, SEQS_LOCAL), HOT),
            pltpu.VMEM((COLS, SEQS_LOCAL), HOT),
            pltpu.VMEM((CHUNKS, LEFT, CHUNK), F32),
            pltpu.VMEM((x_chunks, 7, ROWS, CHUNK), F32),
            pltpu.VMEM((y_chunks, 6, 40, CHUNK), F32),
            pltpu.VMEM((y_chunks, 4, ROWS, CHUNK), F32),
            pltpu.VMEM((CHUNKS, ROWS, CHUNK), F32),
            pltpu.VMEM((4, 56, LANES), F32),
            pltpu.VMEM((7, 56, LANES), F32),
            pltpu.VMEM((56, LANES), F32),
            pltpu.VMEM((4, 40, LANES), F32),
            pltpu.VMEM((8, 4, 40, LANES), F32),
            pltpu.VMEM((4, 16, LANES), F32),
            pltpu.VMEM((ROWS, PANEL), F32),
            pltpu.VMEM((CHUNKS, PANEL, CHUNK), F32),
            pltpu.SemaphoreType.DMA((SEQS_LOCAL // LOAD,)),
            pltpu.SemaphoreType.DMA((N_COPIES,)),
            pltpu.SemaphoreType.DMA((N_COPIES,)),
        ],
        compiler_params=pltpu.CompilerParams(
            collective_id=0, has_side_effects=True, vmem_limit_bytes=56 * 2**20
        ),
        name="couplings",
    )(alignment, cluster_sizes.reshape(SEQS_LOCAL // LANES, LANES), block_inverse)


def solution(mesh):
    in_specs = (P("seq", None), P("seq"), P())
    out_specs = P(("seq", "row"), "col")
    return jax.shard_map(shards, mesh=mesh, in_specs=in_specs, out_specs=out_specs, check_vma=False)
```

```python
import jax
import jax.numpy as jnp
from jax import lax
from jax.experimental import pallas as pl
from jax.experimental.pallas import tpu as pltpu
from jax.sharding import PartitionSpec as P

Q = 20
POS = 256
PANEL = 128
SEQS_LOCAL = 4096
ROWS = 80
COLS = 1280
MAIN = 640
LOAD = 512
LANES = 128
HOT = jnp.float8_e4m3fn
F32 = jnp.float32
MESH = pl.DeviceIdType.MESH
WIDTH = 256
CHUNKS = COLS // WIDTH
HALF = ROWS * 4
LEFT = 2 * HALF + 32
LEFT_MERGED = HALF + 32
N_COPIES = 96
HIGHEST = lax.Precision.HIGHEST
CONTRACT_LAST = (((1,), (1,)), ((), ()))


def position_of(feature):
    return (feature * 3277) >> 16


def hot_rows(state_row, value):
    lanes = LANES
    row = lax.broadcasted_iota(jnp.int32, (8, lanes), 0).astype(F32)
    parts = []
    for tile in range(Q):
        low = 8 * tile
        first, last = low // Q, (low + 7) // Q
        base = float(low - Q * first)
        states = jnp.broadcast_to(state_row(first), (8, lanes))
        level = row + base
        if last != first:
            cut = float(Q * last - low)
            before = row < cut
            states = jnp.where(before, states, jnp.broadcast_to(state_row(last), (8, lanes)))
            level = jnp.where(before, level, row - cut)
        parts.append(jnp.where(states == level, value, 0.0))
    return jnp.concatenate(parts, 0)


def kernel(
    align_hbm, sizes_ref, inverse_ref, out_ref,
    align, states, other, other_sizes, left, left_other, right, right_other,
    first, xr, pairs, yr, final, eu, er, es, mc, pc, pr, panel_cov,
    load_sem, send_sem, recv_sem,
):
    s = lax.axis_index("seq")
    r = lax.axis_index("row")
    c = lax.axis_index("col")
    yh, x = s // 4, s % 4
    x_next, x_far, x_prev = (x + 1) % 4, (x + 2) % 4, (x + 3) % 4
    odd = r % 2
    core = c % 2

    def load(i):
        rows = pl.ds(pl.multiple_of(i * LOAD, LOAD), LOAD)
        return pltpu.make_async_copy(align_hbm.at[rows, :], align.at[rows, :], load_sem.at[i])

    for i in range(SEQS_LOCAL // LOAD):
        load(i).start()

    def at_seq(dx, dy):
        return (((yh + dy) % 2) * 4 + (x + dx) % 4, r, c)

    def at_z(dz):
        return (s, (r + dz) % 8, c)

    z_mate = (s, r + 1 - 2 * odd, c)
    core_mate = (s, r, c + 1 - 2 * core)

    barrier = pltpu.get_barrier_semaphore()

    def greet(peer):
        pl.semaphore_signal(barrier, inc=1, device_id=peer, device_id_type=MESH)

    peers = [at_seq(dx, dy) for dx in range(4) for dy in range(2) if dx or dy]
    peers += [at_z(dz) for dz in (1, 2, 6, 7)]
    peers += [(s, r, (c + dc) % 4) for dc in range(1, 4)]
    for peer in peers:
        greet(peer)
    own_source = [jnp.logical_and(c == 0, s == b) for b in range(2)]
    for b in range(2):
        @pl.when(jnp.logical_not(own_source[b]))
        def _():
            greet((2 * c + b, r, 0))

    used = []
    sends = []

    def reserve(count):
        low = len(used)
        used.extend(range(low, low + count))
        return low

    def copy_at(index, src, dst, device):
        return pltpu.make_async_remote_copy(
            src_ref=src, dst_ref=dst, send_sem=send_sem.at[index], recv_sem=recv_sem.at[index],
            device_id=device, device_id_type=MESH,
        )

    def push(src, dst, device):
        copy = copy_at(reserve(1), src, dst, device)
        copy.start()
        sends.append(copy)
        return copy

    row_id = lax.broadcasted_iota(jnp.int32, (96, POS), 0)
    pos_id = lax.broadcasted_iota(jnp.int32, (96, POS), 1)
    half_id = jnp.where(row_id < 16, yh, 1 - yh)
    wanted = jnp.where(
        row_id < 32,
        half_id * 128 + ((row_id >> 2) & 3) * 32 + r * 4 + (row_id & 3),
        c * 64 + row_id - 32,
    )
    pick = (pos_id == wanted).astype(F32).astype(jnp.bfloat16)
    first_row = lax.broadcasted_iota(jnp.int32, (32, LANES), 0) == 0

    @pl.loop(0, SEQS_LOCAL // LOAD)
    def _(i):
        load(i).wait()
        span = pl.ds(pl.multiple_of(i * LOAD, LOAD), LOAD)
        block = align[span, :].astype(F32).astype(jnp.bfloat16)
        found = lax.dot_general(pick, block, CONTRACT_LAST, preferred_element_type=F32)
        for g in range(12):
            states[g, :, span] = found[8 * g:8 * g + 8]

    pl.semaphore_wait(barrier, len(peers) + jnp.where(c == 0, jnp.where(s < 2, 7, 8), 0))
    size_copy = push(sizes_ref, other_sizes, at_seq(0, 1))
    row_half = push(states.at[2 + core], other.at[core], at_seq(0, 1))
    y_base = reserve(4)
    z_base = reserve(4)

    def y_block(i):
        return 2 * i + 2 - odd

    def z_block(i):
        return 2 * i + 1 + odd

    def other_rows(b):
        return other.at[2 + b]

    def y_copy(i):
        b = y_block(i)
        return copy_at(y_base + i, states.at[4 + b], other_rows(b), at_seq(0, 1))

    def z_copy(i):
        return copy_at(z_base + i, other_rows(y_block(i)), other_rows(y_block(i)), z_mate)

    def z_arrival(i):
        return copy_at(z_base + i, other_rows(z_block(i)), other_rows(z_block(i)), z_mate)

    for i in range(3):
        y_copy(i).start()

    @pl.when(odd == 1)
    def _():
        y_copy(3).start()

    def hot_right(target, source, group, b, lanes):
        rows = pl.ds(160 * b, 160) if isinstance(b, int) else pl.ds(pl.multiple_of(160 * b, 160), 160)
        target[rows, lanes] = hot_rows(
            lambda p: source[group + b, pl.ds(p, 1), lanes], 1.0
        ).astype(HOT)

    def hot_left(target, low, source, group, blocks, weight, lanes):
        weight8 = jnp.broadcast_to(weight, (8, LANES))
        for b in range(blocks):
            target[pl.ds(low + 160 * b, 160), lanes] = hot_rows(
                lambda p: source[group + b, pl.ds(p, 1), lanes], weight8
            ).astype(HOT)

    def weight_rows(weight):
        return jnp.where(first_row, jnp.broadcast_to(weight, (32, LANES)), 0.0).astype(HOT)

    def lanes_at(i):
        return pl.ds(pl.multiple_of(i * LANES, LANES), LANES)

    @pl.loop(0, SEQS_LOCAL // LANES)
    def _(i):
        lanes = lanes_at(i)
        weight = 1.0 / sizes_ref[pl.ds(i, 1), :].astype(F32)
        hot_left(left, 0, states, 0, 2, weight, lanes)
        left[pl.ds(HALF, 32), lanes] = weight_rows(weight)
        hot_left(left, LEFT_MERGED, states, 2, 2, weight, lanes)
        for b in range(2):
            hot_right(right, states, 4, b, lanes)

    first[...] = lax.dot_general(
        left[...], right[pl.ds(0, WIDTH), :], CONTRACT_LAST, preferred_element_type=F32
    )

    def first_block(other_half, to_x):
        start = other_half * LEFT_MERGED + to_x * ROWS
        return first.at[pl.ds(pl.multiple_of(start, 8), ROWS), :]

    first_copies = [
        push(first_block(0, x_far), xr.at[0], at_seq(1, 0)),
        push(first_block(1, x_far), xr.at[1], at_seq(3, 0)),
        push(first_block(1, x_next), xr.at[2], at_seq(1, 0)),
        push(first_block(0, x_prev), xr.at[3], at_seq(3, 0)),
    ]
    @pl.loop(0, SEQS_LOCAL // LANES)
    def _(i):
        for b in range(2, 8):
            hot_right(right, states, 4, b, lanes_at(i))

    def hot_other(b):
        @pl.loop(0, SEQS_LOCAL // LANES)
        def _(i):
            hot_right(right_other, other, 2, b, lanes_at(i))

    def finish_first():
        first_copies[6].wait_recv()
        return first_block(0, x)[...] + xr[6]

    def multiply(j):
        rows = pl.ds(j * WIDTH, WIDTH)
        pairs[j - 1] = lax.dot_general(
            left[pl.ds(0, LEFT_MERGED), :], right[rows, :], CONTRACT_LAST, preferred_element_type=F32
        )

    def multiply_other(j):
        rows = pl.ds(j * WIDTH, WIDTH)
        pairs[j - 1, pl.ds(0, HALF), :] += lax.dot_general(
            left_other[...], right_other[rows, :], CONTRACT_LAST, preferred_element_type=F32
        )

    def part(j, to_x, low):
        return pairs.at[j - 1, pl.ds(pl.multiple_of(to_x * ROWS + low, 8), 40), :]

    copies = {}

    def stage_one(j):
        copies[j] = [
            push(part(j, x_far, 0), yr.at[j - 1, 0], at_seq(1, 0)),
            push(part(j, x_far, 40), yr.at[j - 1, 1], at_seq(3, 0)),
            push(part(j, x_next, 40), yr.at[j - 1, 2], at_seq(1, 0)),
            push(part(j, x_prev, 0), yr.at[j - 1, 3], at_seq(3, 0)),
        ]

    def stage_two(j):
        done = copies[j]
        done[0].wait_recv()
        part(j, x_next, 0)[...] += yr[j - 1, 0]
        done.append(push(part(j, x_next, 0), yr.at[j - 1, 4], at_seq(1, 0)))
        done[1].wait_recv()
        part(j, x_prev, 40)[...] += yr[j - 1, 1]
        done.append(push(part(j, x_prev, 40), yr.at[j - 1, 5], at_seq(3, 0)))

    def finish(j):
        for i in range(2, 6):
            copies[j][i].wait_recv()
        top = part(j, x, 0)[...] + yr[j - 1, 4] + yr[j - 1, 3]
        bottom = part(j, x, 40)[...] + yr[j - 1, 2] + yr[j - 1, 5]
        return jnp.concatenate([top, bottom], 0)

    row_half.wait_recv()
    row_share = push(other.at[core], other.at[core], core_mate)
    multiply(1)
    multiply(2)
    first_copies[0].wait_recv()
    first_block(0, x_next)[...] += xr[0]
    first_copies.append(push(first_block(0, x_next), xr.at[4], at_seq(1, 0)))
    first_copies[1].wait_recv()
    first_block(1, x_prev)[...] += xr[1]
    first_copies.append(push(first_block(1, x_prev), xr.at[5], at_seq(3, 0)))
    y_copy(0).wait_recv()
    z_copy(0).start()
    multiply(3)
    multiply(4)
    weight_sum = jnp.sum(
        jnp.sum(1.0 / sizes_ref[...].astype(F32), axis=0, keepdims=True), axis=1, keepdims=True
    )
    for tile in range(10):
        j, lanes = tile // 2, pl.ds((tile % 2) * LANES, LANES)
        eu[pl.ds(tile, 1), :] = (first if j == 0 else pairs.at[j - 1])[pl.ds(HALF, 1), lanes]
    eu[pl.ds(10, 6), :] = jnp.broadcast_to(weight_sum, (6, LANES))
    margin_sums = []
    for dx in range(4):
        for dy in range(2):
            if dx or dy:
                margin_sums.append(push(eu, er.at[dx * 2 + dy - 1], at_seq(dx, dy)))
    row_share.wait_recv()
    size_copy.wait_recv()

    @pl.loop(0, SEQS_LOCAL // LANES)
    def _(i):
        lanes = lanes_at(i)
        weight = 1.0 / other_sizes[pl.ds(i, 1), :].astype(F32)
        hot_left(left_other, 0, other, 0, 2, weight, lanes)

    for i in range(2, 6):
        first_copies[i].wait_recv()
    first_block(0, x)[...] += xr[4] + xr[3]
    first_block(1, x)[...] += xr[2] + xr[5]
    first_copies.append(push(first_block(1, x), xr.at[6], at_seq(0, 1)))
    y_copy(1).wait_recv()
    z_copy(1).start()
    hot_other(y_block(0))
    z_arrival(0).wait_recv()
    hot_other(z_block(0))
    y_copy(2).wait_recv()
    z_copy(2).start()
    hot_other(y_block(1))
    final[...] = finish_first()
    base = reserve(11)

    def panel_copy(i):
        return pltpu.make_async_remote_copy(
            src_ref=final.at[:, pl.ds(0, PANEL)], dst_ref=pc.at[s % 2, r],
            send_sem=send_sem.at[base + i], recv_sem=recv_sem.at[base + s % 2],
            device_id=(((yh + i // 4) % 2) * 4 + (x + i % 4) % 4, r, s // 2), device_id_type=MESH,
        )

    def panel_arrival(b):
        return pltpu.make_async_remote_copy(
            src_ref=final.at[:, pl.ds(0, PANEL)], dst_ref=pc.at[b, r],
            send_sem=send_sem.at[base], recv_sem=recv_sem.at[base + b],
            device_id=at_seq(1, 0), device_id_type=MESH,
        )

    def row_copy(i):
        return pltpu.make_async_remote_copy(
            src_ref=final.at[:, pl.ds(0, PANEL)], dst_ref=pr,
            send_sem=send_sem.at[base + 8 + i], recv_sem=recv_sem.at[base + 8],
            device_id=(s, r, (c + 1 + i) % 4), device_id_type=MESH,
        )

    sends_panel = c == 0
    to_itself = jnp.logical_and(sends_panel, s < 2)
    to_another = jnp.logical_and(sends_panel, s >= 2)

    @pl.when(sends_panel)
    def _():
        for i in range(1, 8):
            panel_copy(i).start()

    @pl.when(to_another)
    def _():
        panel_copy(0).start()

    @pl.when(to_itself)
    def _():
        pc[s % 2, r] = final[:, pl.ds(0, PANEL)]

    @pl.when(sends_panel)
    def _():
        for i in range(3):
            row_copy(i).start()
        pr[...] = final[:, pl.ds(0, PANEL)]

    z_arrival(1).wait_recv()
    hot_other(z_block(1))

    @pl.when(odd == 1)
    def _():
        y_copy(3).wait_recv()
        z_copy(3).start()

    multiply_other(1)
    stage_one(1)
    multiply_other(2)
    stage_one(2)
    hot_other(y_block(2))
    z_arrival(2).wait_recv()
    hot_other(z_block(2))
    stage_two(1)
    multiply_other(3)
    stage_one(3)

    total = eu[...]
    for i in range(7):
        margin_sums[i].wait_recv()
        total = total + er[i]
    es[...] = total
    mc[c] = total
    margin_gathers = [push(es, mc.at[c], (s, r, (c + dc) % 4)) for dc in range(1, 4)]
    for b in range(2):
        @pl.when(jnp.logical_not(own_source[b]))
        def _():
            panel_arrival(b).wait_recv()

    z_copies = [push(pc.at[:, r], pc.at[:, r], at_z(dz)) for dz in (2, 6, 1, 7)]
    @pl.when(odd == 0)
    def _():
        z_arrival(3).wait_recv()

    hot_other(7)
    stage_two(2)
    multiply_other(4)
    stage_one(4)
    stage_two(3)
    low_z, high_z = (r + 6) % 8, (r + 2) % 8
    z_copies[0].wait_recv()
    z_copies.append(push(pc.at[:, low_z], pc.at[:, low_z], at_z(1)))
    z_copies.append(push(pc.at[0, low_z], pc.at[0, low_z], at_z(2)))
    z_copies[1].wait_recv()
    z_copies.append(push(pc.at[:, high_z], pc.at[:, high_z], at_z(7)))
    z_copies.append(push(pc.at[1, high_z], pc.at[1, high_z], at_z(6)))

    @pl.when(c != 0)
    def _():
        row_copy(0).wait_recv()

    for copy in margin_gathers:
        copy.wait_recv()
    half = 0.5 / mc[c, pl.ds(10, 1), :]
    floor = 0.5 / Q
    half_cols = jnp.concatenate([half] * 10, 1)
    col_freq = (
        jnp.concatenate([mc[c, pl.ds(i, 1), :] for i in range(10)], 1) * half_cols + floor
    )
    panel_freq = mc[0, pl.ds(0, 1), :] * half + floor
    row_low = (s * 8 + r) * ROWS
    local = (s % 2) * MAIN + r * ROWS + lax.broadcasted_iota(jnp.int32, (ROWS, LANES), 0)
    lane = lax.broadcasted_iota(jnp.int32, (ROWS, LANES), 1)
    found = jnp.zeros((ROWS, LANES), F32)
    for i in range(10):
        margin = jnp.broadcast_to(mc[s // 2, pl.ds(i, 1), :] * half, (ROWS, LANES))
        found += jnp.where(local == lane + i * LANES, margin, 0.0)
    row_freq = jnp.sum(found, axis=1, keepdims=True) + floor
    eye = lax.broadcasted_iota(jnp.int32, (PANEL, PANEL), 0) == lax.broadcasted_iota(
        jnp.int32, (PANEL, PANEL), 1
    )

    def prior(shape, row_first, col_first):
        row = row_first + lax.broadcasted_iota(jnp.int32, shape, 0)
        col = col_first + lax.broadcasted_iota(jnp.int32, shape, 1)
        return jnp.where(
            position_of(row) == position_of(col),
            jnp.where(row == col, 0.5 / Q, 0.0),
            0.5 / (Q * Q),
        )

    panel_rows = pr[...] * half + prior((ROWS, PANEL), row_low, 0) - row_freq * panel_freq
    symmetric = 0.5 * (inverse_ref[...] + inverse_ref[...].T)
    factor = jnp.dot(panel_rows, symmetric, precision=HIGHEST, preferred_element_type=F32)
    for i in range(10):
        lanes = slice(i * LANES, (i + 1) * LANES)
        freq = jnp.broadcast_to(col_freq[:, lanes], (PANEL, PANEL))
        column = jnp.sum(jnp.where(eye, freq, 0.0), axis=1, keepdims=True)
        panel_cov[pl.ds(i * LANES, LANES), :] = (
            prior((PANEL, PANEL), c * COLS + i * LANES, 0) - column * panel_freq
        )
    for j in range(CHUNKS):
        low, width = j * WIDTH, WIDTH
        shift = prior((ROWS, width), row_low, c * COLS + low)
        shift = shift - row_freq * col_freq[:, low:low + width]
        out_ref[:, pl.ds(low, width)] = -float(Q) * shift
    stage_two(4)
    for copy in z_copies[2:]:
        copy.wait_recv()
    for b in range(2):
        for z in range(8):
            panel_cov[pl.ds((b * 8 + z) * ROWS, ROWS), :] += pc[b, z] * half
    for j in range(CHUNKS):
        low, width = j * WIDTH, WIDTH
        update = lax.dot_general(
            factor, panel_cov[pl.ds(low, width), :], CONTRACT_LAST, precision=HIGHEST,
            preferred_element_type=F32,
        )
        out_ref[:, pl.ds(low, width)] += float(Q) * update
    for j in range(CHUNKS):
        low, width = j * WIDTH, WIDTH
        sums = final[...] if j == 0 else finish(j)
        out_ref[:, pl.ds(low, width)] += sums * (half_cols[:, low:low + width] * -float(Q))

    for copy in sends:
        copy.wait_send()
    for i in range(3):
        y_copy(i).wait_send()
        z_copy(i).wait_send()

    @pl.when(odd == 1)
    def _():
        y_copy(3).wait_send()
        z_copy(3).wait_send()

    @pl.when(sends_panel)
    def _():
        for i in range(1, 8):
            panel_copy(i).wait_send()
        for i in range(3):
            row_copy(i).wait_send()

    @pl.when(to_another)
    def _():
        panel_copy(0).wait_send()

    assert len(used) <= N_COPIES


def shards(alignment, cluster_sizes, block_inverse):
    vmem = pl.BlockSpec(memory_space=pltpu.VMEM)

    return pl.pallas_call(
        kernel,
        out_shape=jax.ShapeDtypeStruct((ROWS, COLS), F32),
        in_specs=[pl.BlockSpec(memory_space=pl.ANY), vmem, vmem],
        out_specs=vmem,
        scratch_shapes=[
            pltpu.VMEM((SEQS_LOCAL, POS), jnp.int32),
            pltpu.VMEM((12, 8, SEQS_LOCAL), F32),
            pltpu.VMEM((10, 8, SEQS_LOCAL), F32),
            pltpu.VMEM((SEQS_LOCAL // LANES, LANES), jnp.int32),
            pltpu.VMEM((LEFT, SEQS_LOCAL), HOT),
            pltpu.VMEM((HALF, SEQS_LOCAL), HOT),
            pltpu.VMEM((COLS, SEQS_LOCAL), HOT),
            pltpu.VMEM((COLS, SEQS_LOCAL), HOT),
            pltpu.VMEM((LEFT, WIDTH), F32),
            pltpu.VMEM((7, ROWS, WIDTH), F32),
            pltpu.VMEM((CHUNKS - 1, LEFT_MERGED, WIDTH), F32),
            pltpu.VMEM((CHUNKS - 1, 6, 40, WIDTH), F32),
            pltpu.VMEM((ROWS, WIDTH), F32),
            pltpu.VMEM((16, LANES), F32),
            pltpu.VMEM((7, 16, LANES), F32),
            pltpu.VMEM((16, LANES), F32),
            pltpu.VMEM((4, 16, LANES), F32),
            pltpu.VMEM((2, 8, ROWS, PANEL), F32),
            pltpu.VMEM((ROWS, PANEL), F32),
            pltpu.VMEM((COLS, PANEL), F32),
            pltpu.SemaphoreType.DMA((SEQS_LOCAL // LOAD,)),
            pltpu.SemaphoreType.DMA((N_COPIES,)),
            pltpu.SemaphoreType.DMA((N_COPIES,)),
        ],
        compiler_params=pltpu.CompilerParams(
            collective_id=0, has_side_effects=True, vmem_limit_bytes=56 * 2**20
        ),
        name="couplings",
    )(alignment, cluster_sizes.reshape(SEQS_LOCAL // LANES, LANES), block_inverse)


def solution(mesh):
    in_specs = (P("seq", None), P("seq"), P())
    out_specs = P(("seq", "row"), "col")
    return jax.shard_map(shards, mesh=mesh, in_specs=in_specs, out_specs=out_specs, check_vma=False)
```

```python
import jax
import jax.numpy as jnp
from jax import lax
from jax.experimental import pallas as pl
from jax.experimental.pallas import tpu as pltpu
from jax.sharding import PartitionSpec as P

Q = 20
POS = 256
PANEL = 128
SEQS_LOCAL = 4096
ROWS = 80
COLS = 1280
MAIN = 640
LOAD = 512
LANES = 128
HOT = jnp.float8_e4m3fn
F32 = jnp.float32
MESH = pl.DeviceIdType.MESH
WIDTH = 256
CHUNKS = COLS // WIDTH
HALF = ROWS * 4
LEFT = 2 * HALF + 32
LEFT_MERGED = HALF + 32
N_COPIES = 96
HIGHEST = lax.Precision.HIGHEST
CONTRACT_LAST = (((1,), (1,)), ((), ()))


def position_of(feature):
    return (feature * 3277) >> 16


def hot_rows(state_row, value):
    lanes = LANES
    row = lax.broadcasted_iota(jnp.int32, (8, lanes), 0).astype(F32)
    parts = []
    for tile in range(Q):
        low = 8 * tile
        first, last = low // Q, (low + 7) // Q
        base = float(low - Q * first)
        states = jnp.broadcast_to(state_row(first), (8, lanes))
        level = row + base
        if last != first:
            cut = float(Q * last - low)
            before = row < cut
            states = jnp.where(before, states, jnp.broadcast_to(state_row(last), (8, lanes)))
            level = jnp.where(before, level, row - cut)
        parts.append(jnp.where(states == level, value, 0.0))
    return jnp.concatenate(parts, 0)


def kernel(
    align_hbm, sizes_ref, inverse_ref, out_ref,
    align, states, other, other_sizes, left, left_other, right, right_other,
    first, xr, pairs, yr, final, eu, er, es, mc, pc, pr, panel_cov,
    load_sem, send_sem, recv_sem,
):
    s = lax.axis_index("seq")
    r = lax.axis_index("row")
    c = lax.axis_index("col")
    yh, x = s // 4, s % 4
    x_next, x_far, x_prev = (x + 1) % 4, (x + 2) % 4, (x + 3) % 4
    odd = r % 2
    core = c % 2

    def load(i):
        rows = pl.ds(pl.multiple_of(i * LOAD, LOAD), LOAD)
        return pltpu.make_async_copy(align_hbm.at[rows, :], align.at[rows, :], load_sem.at[i])

    for i in range(SEQS_LOCAL // LOAD):
        load(i).start()

    def at_seq(dx, dy):
        return (((yh + dy) % 2) * 4 + (x + dx) % 4, r, c)

    def at_z(dz):
        return (s, (r + dz) % 8, c)

    z_mate = (s, r + 1 - 2 * odd, c)
    core_mate = (s, r, c + 1 - 2 * core)

    barrier = pltpu.get_barrier_semaphore()

    def greet(peer):
        pl.semaphore_signal(barrier, inc=1, device_id=peer, device_id_type=MESH)

    peers = [at_seq(dx, dy) for dx in range(4) for dy in range(2) if dx or dy]
    peers += [at_z(dz) for dz in (1, 2, 6, 7)]
    peers += [(s, r, (c + dc) % 4) for dc in range(1, 4)]
    for peer in peers:
        greet(peer)
    own_source = [jnp.logical_and(c == 0, s == b) for b in range(2)]
    for b in range(2):
        @pl.when(jnp.logical_not(own_source[b]))
        def _():
            greet((2 * c + b, r, 0))

    used = []
    sends = []

    def reserve(count):
        low = len(used)
        used.extend(range(low, low + count))
        return low

    def copy_at(index, src, dst, device):
        return pltpu.make_async_remote_copy(
            src_ref=src, dst_ref=dst, send_sem=send_sem.at[index], recv_sem=recv_sem.at[index],
            device_id=device, device_id_type=MESH,
        )

    def push(src, dst, device):
        copy = copy_at(reserve(1), src, dst, device)
        copy.start()
        sends.append(copy)
        return copy

    row_id = lax.broadcasted_iota(jnp.int32, (96, POS), 0)
    pos_id = lax.broadcasted_iota(jnp.int32, (96, POS), 1)
    half_id = jnp.where(row_id < 16, yh, 1 - yh)
    wanted = jnp.where(
        row_id < 32,
        half_id * 128 + ((row_id >> 2) & 3) * 32 + r * 4 + (row_id & 3),
        c * 64 + row_id - 32,
    )
    pick = (pos_id == wanted).astype(F32).astype(jnp.bfloat16)
    first_row = lax.broadcasted_iota(jnp.int32, (32, LANES), 0) == 0

    @pl.loop(0, SEQS_LOCAL // LOAD)
    def _(i):
        load(i).wait()
        span = pl.ds(pl.multiple_of(i * LOAD, LOAD), LOAD)
        block = align[span, :].astype(F32).astype(jnp.bfloat16)
        found = lax.dot_general(pick, block, CONTRACT_LAST, preferred_element_type=F32)
        for g in range(12):
            states[g, :, span] = found[8 * g:8 * g + 8]

    pl.semaphore_wait(barrier, len(peers) + jnp.where(c == 0, jnp.where(s < 2, 7, 8), 0))
    size_copy = push(sizes_ref, other_sizes, at_seq(0, 1))
    row_half = push(states.at[2 + core], other.at[core], at_seq(0, 1))
    y_base = reserve(4)
    z_base = reserve(4)

    def y_block(i):
        return 2 * i + 2 - odd

    def z_block(i):
        return 2 * i + 1 + odd

    def other_rows(b):
        return other.at[2 + b]

    def y_copy(i):
        b = y_block(i)
        return copy_at(y_base + i, states.at[4 + b], other_rows(b), at_seq(0, 1))

    def z_copy(i):
        return copy_at(z_base + i, other_rows(y_block(i)), other_rows(y_block(i)), z_mate)

    def z_arrival(i):
        return copy_at(z_base + i, other_rows(z_block(i)), other_rows(z_block(i)), z_mate)

    for i in range(3):
        y_copy(i).start()

    @pl.when(odd == 1)
    def _():
        y_copy(3).start()

    def hot_right(target, source, group, b, lanes):
        rows = pl.ds(160 * b, 160) if isinstance(b, int) else pl.ds(pl.multiple_of(160 * b, 160), 160)
        target[rows, lanes] = hot_rows(
            lambda p: source[group + b, pl.ds(p, 1), lanes], 1.0
        ).astype(HOT)

    def hot_left(target, low, source, group, blocks, weight, lanes):
        weight8 = jnp.broadcast_to(weight, (8, LANES))
        for b in range(blocks):
            target[pl.ds(low + 160 * b, 160), lanes] = hot_rows(
                lambda p: source[group + b, pl.ds(p, 1), lanes], weight8
            ).astype(HOT)

    def weight_rows(weight):
        return jnp.where(first_row, jnp.broadcast_to(weight, (32, LANES)), 0.0).astype(HOT)

    def lanes_at(i):
        return pl.ds(pl.multiple_of(i * LANES, LANES), LANES)

    @pl.loop(0, SEQS_LOCAL // LANES)
    def _(i):
        lanes = lanes_at(i)
        weight = 1.0 / sizes_ref[pl.ds(i, 1), :].astype(F32)
        hot_left(left, 0, states, 0, 2, weight, lanes)
        left[pl.ds(HALF, 32), lanes] = weight_rows(weight)
        hot_left(left, LEFT_MERGED, states, 2, 2, weight, lanes)
        for b in range(2):
            hot_right(right, states, 4, b, lanes)

    first[...] = lax.dot_general(
        left[...], right[pl.ds(0, WIDTH), :], CONTRACT_LAST, preferred_element_type=F32
    )

    def first_block(other_half, to_x):
        start = other_half * LEFT_MERGED + to_x * ROWS
        return first.at[pl.ds(pl.multiple_of(start, 8), ROWS), :]

    first_copies = [
        push(first_block(0, x_far), xr.at[0], at_seq(1, 0)),
        push(first_block(1, x_far), xr.at[1], at_seq(3, 0)),
        push(first_block(1, x_next), xr.at[2], at_seq(1, 0)),
        push(first_block(0, x_prev), xr.at[3], at_seq(3, 0)),
    ]
    @pl.loop(0, SEQS_LOCAL // LANES)
    def _(i):
        for b in range(2, 8):
            hot_right(right, states, 4, b, lanes_at(i))

    def hot_other(b):
        @pl.loop(0, SEQS_LOCAL // LANES)
        def _(i):
            hot_right(right_other, other, 2, b, lanes_at(i))

    def finish_first():
        first_copies[6].wait_recv()
        return first_block(0, x)[...] + xr[6]

    def multiply(j):
        rows = pl.ds(j * WIDTH, WIDTH)
        pairs[j - 1] = lax.dot_general(
            left[pl.ds(0, LEFT_MERGED), :], right[rows, :], CONTRACT_LAST, preferred_element_type=F32
        )

    def multiply_other(j):
        rows = pl.ds(j * WIDTH, WIDTH)
        pairs[j - 1, pl.ds(0, HALF), :] += lax.dot_general(
            left_other[...], right_other[rows, :], CONTRACT_LAST, preferred_element_type=F32
        )

    def part(j, to_x, low):
        return pairs.at[j - 1, pl.ds(pl.multiple_of(to_x * ROWS + low, 8), 40), :]

    copies = {}

    def stage_one(j):
        copies[j] = [
            push(part(j, x_far, 0), yr.at[j - 1, 0], at_seq(1, 0)),
            push(part(j, x_far, 40), yr.at[j - 1, 1], at_seq(3, 0)),
            push(part(j, x_next, 40), yr.at[j - 1, 2], at_seq(1, 0)),
            push(part(j, x_prev, 0), yr.at[j - 1, 3], at_seq(3, 0)),
        ]

    def stage_two(j):
        done = copies[j]
        done[0].wait_recv()
        part(j, x_next, 0)[...] += yr[j - 1, 0]
        done.append(push(part(j, x_next, 0), yr.at[j - 1, 4], at_seq(1, 0)))
        done[1].wait_recv()
        part(j, x_prev, 40)[...] += yr[j - 1, 1]
        done.append(push(part(j, x_prev, 40), yr.at[j - 1, 5], at_seq(3, 0)))

    def finish(j):
        for i in range(2, 6):
            copies[j][i].wait_recv()
        top = part(j, x, 0)[...] + yr[j - 1, 4] + yr[j - 1, 3]
        bottom = part(j, x, 40)[...] + yr[j - 1, 2] + yr[j - 1, 5]
        return jnp.concatenate([top, bottom], 0)

    row_half.wait_recv()
    row_share = push(other.at[core], other.at[core], core_mate)
    multiply(1)
    multiply(2)
    first_copies[0].wait_recv()
    first_block(0, x_next)[...] += xr[0]
    first_copies.append(push(first_block(0, x_next), xr.at[4], at_seq(1, 0)))
    first_copies[1].wait_recv()
    first_block(1, x_prev)[...] += xr[1]
    first_copies.append(push(first_block(1, x_prev), xr.at[5], at_seq(3, 0)))
    y_copy(0).wait_recv()
    z_copy(0).start()
    multiply(3)
    multiply(4)
    weight_sum = jnp.sum(
        jnp.sum(1.0 / sizes_ref[...].astype(F32), axis=0, keepdims=True), axis=1, keepdims=True
    )
    for tile in range(10):
        j, lanes = tile // 2, pl.ds((tile % 2) * LANES, LANES)
        eu[pl.ds(tile, 1), :] = (first if j == 0 else pairs.at[j - 1])[pl.ds(HALF, 1), lanes]
    eu[pl.ds(10, 6), :] = jnp.broadcast_to(weight_sum, (6, LANES))
    margin_sums = []
    for dx in range(4):
        for dy in range(2):
            if dx or dy:
                margin_sums.append(push(eu, er.at[dx * 2 + dy - 1], at_seq(dx, dy)))
    row_share.wait_recv()
    size_copy.wait_recv()

    @pl.loop(0, SEQS_LOCAL // LANES)
    def _(i):
        lanes = lanes_at(i)
        weight = 1.0 / other_sizes[pl.ds(i, 1), :].astype(F32)
        hot_left(left_other, 0, other, 0, 2, weight, lanes)

    for i in range(2, 6):
        first_copies[i].wait_recv()
    first_block(0, x)[...] += xr[4] + xr[3]
    first_block(1, x)[...] += xr[2] + xr[5]
    first_copies.append(push(first_block(1, x), xr.at[6], at_seq(0, 1)))
    y_copy(1).wait_recv()
    z_copy(1).start()
    hot_other(y_block(0))
    z_arrival(0).wait_recv()
    hot_other(z_block(0))
    y_copy(2).wait_recv()
    z_copy(2).start()
    hot_other(y_block(1))
    final[...] = finish_first()
    base = reserve(11)

    def panel_copy(i):
        return pltpu.make_async_remote_copy(
            src_ref=final.at[:, pl.ds(0, PANEL)], dst_ref=pc.at[s % 2, r],
            send_sem=send_sem.at[base + i], recv_sem=recv_sem.at[base + s % 2],
            device_id=(((yh + i // 4) % 2) * 4 + (x + i % 4) % 4, r, s // 2), device_id_type=MESH,
        )

    def panel_arrival(b):
        return pltpu.make_async_remote_copy(
            src_ref=final.at[:, pl.ds(0, PANEL)], dst_ref=pc.at[b, r],
            send_sem=send_sem.at[base], recv_sem=recv_sem.at[base + b],
            device_id=at_seq(1, 0), device_id_type=MESH,
        )

    def row_copy(i):
        return pltpu.make_async_remote_copy(
            src_ref=final.at[:, pl.ds(0, PANEL)], dst_ref=pr,
            send_sem=send_sem.at[base + 8 + i], recv_sem=recv_sem.at[base + 8],
            device_id=(s, r, (c + 1 + i) % 4), device_id_type=MESH,
        )

    sends_panel = c == 0
    to_itself = jnp.logical_and(sends_panel, s < 2)
    to_another = jnp.logical_and(sends_panel, s >= 2)

    @pl.when(sends_panel)
    def _():
        for i in range(1, 8):
            panel_copy(i).start()

    @pl.when(to_another)
    def _():
        panel_copy(0).start()

    @pl.when(to_itself)
    def _():
        pc[s % 2, r] = final[:, pl.ds(0, PANEL)]

    @pl.when(sends_panel)
    def _():
        for i in range(3):
            row_copy(i).start()
        pr[...] = final[:, pl.ds(0, PANEL)]

    z_arrival(1).wait_recv()
    hot_other(z_block(1))

    @pl.when(odd == 1)
    def _():
        y_copy(3).wait_recv()
        z_copy(3).start()

    multiply_other(1)
    stage_one(1)
    multiply_other(2)
    stage_one(2)
    hot_other(y_block(2))
    z_arrival(2).wait_recv()
    hot_other(z_block(2))
    stage_two(1)
    multiply_other(3)
    stage_one(3)

    total = eu[...]
    for i in range(7):
        margin_sums[i].wait_recv()
        total = total + er[i]
    es[...] = total
    mc[c] = total
    margin_gathers = [push(es, mc.at[c], (s, r, (c + dc) % 4)) for dc in range(1, 4)]
    for b in range(2):
        @pl.when(jnp.logical_not(own_source[b]))
        def _():
            panel_arrival(b).wait_recv()

    z_copies = [push(pc.at[:, r], pc.at[:, r], at_z(dz)) for dz in (2, 6, 1, 7)]
    @pl.when(odd == 0)
    def _():
        z_arrival(3).wait_recv()

    hot_other(7)
    stage_two(2)
    multiply_other(4)
    stage_one(4)
    stage_two(3)
    low_z, high_z = (r + 6) % 8, (r + 2) % 8
    z_copies[0].wait_recv()
    z_copies.append(push(pc.at[:, low_z], pc.at[:, low_z], at_z(1)))
    z_copies.append(push(pc.at[0, low_z], pc.at[0, low_z], at_z(2)))
    z_copies[1].wait_recv()
    z_copies.append(push(pc.at[:, high_z], pc.at[:, high_z], at_z(7)))
    z_copies.append(push(pc.at[1, high_z], pc.at[1, high_z], at_z(6)))

    @pl.when(c != 0)
    def _():
        row_copy(0).wait_recv()

    for copy in margin_gathers:
        copy.wait_recv()
    half = 0.5 / mc[c, pl.ds(10, 1), :]
    floor = 0.5 / Q
    half_cols = jnp.concatenate([half] * 10, 1)
    col_freq = (
        jnp.concatenate([mc[c, pl.ds(i, 1), :] for i in range(10)], 1) * half_cols + floor
    )
    panel_freq = mc[0, pl.ds(0, 1), :] * half + floor
    row_low = (s * 8 + r) * ROWS
    local = (s % 2) * MAIN + r * ROWS + lax.broadcasted_iota(jnp.int32, (ROWS, LANES), 0)
    lane = lax.broadcasted_iota(jnp.int32, (ROWS, LANES), 1)
    found = jnp.zeros((ROWS, LANES), F32)
    for i in range(10):
        margin = jnp.broadcast_to(mc[s // 2, pl.ds(i, 1), :] * half, (ROWS, LANES))
        found += jnp.where(local == lane + i * LANES, margin, 0.0)
    row_freq = jnp.sum(found, axis=1, keepdims=True) + floor
    eye = lax.broadcasted_iota(jnp.int32, (PANEL, PANEL), 0) == lax.broadcasted_iota(
        jnp.int32, (PANEL, PANEL), 1
    )

    def prior(shape, row_first, col_first):
        row = row_first + lax.broadcasted_iota(jnp.int32, shape, 0)
        col = col_first + lax.broadcasted_iota(jnp.int32, shape, 1)
        return jnp.where(
            position_of(row) == position_of(col),
            jnp.where(row == col, 0.5 / Q, 0.0),
            0.5 / (Q * Q),
        )

    panel_rows = pr[...] * half + prior((ROWS, PANEL), row_low, 0) - row_freq * panel_freq
    symmetric = 0.5 * (inverse_ref[...] + inverse_ref[...].T)
    factor = jnp.dot(panel_rows, symmetric, precision=HIGHEST, preferred_element_type=F32)
    for i in range(10):
        lanes = slice(i * LANES, (i + 1) * LANES)
        freq = jnp.broadcast_to(col_freq[:, lanes], (PANEL, PANEL))
        column = jnp.sum(jnp.where(eye, freq, 0.0), axis=1, keepdims=True)
        panel_cov[pl.ds(i * LANES, LANES), :] = (
            prior((PANEL, PANEL), c * COLS + i * LANES, 0) - column * panel_freq
        )
    for j in range(CHUNKS):
        low, width = j * WIDTH, WIDTH
        shift = prior((ROWS, width), row_low, c * COLS + low)
        shift = shift - row_freq * col_freq[:, low:low + width]
        out_ref[:, pl.ds(low, width)] = -float(Q) * shift
    stage_two(4)
    def halves(value):
        high = value.astype(jnp.bfloat16)
        return high, (value - high.astype(F32)).astype(jnp.bfloat16)

    factor_high, factor_low = halves(factor)
    factor_parts = jnp.concatenate([factor_high, factor_low, factor_high], 1)
    for copy in z_copies[2:]:
        copy.wait_recv()
    for b in range(2):
        for z in range(8):
            panel_cov[pl.ds((b * 8 + z) * ROWS, ROWS), :] += pc[b, z] * half
    for j in range(CHUNKS):
        low, width = j * WIDTH, WIDTH
        high, low_part = halves(panel_cov[pl.ds(low, width), :])
        update = lax.dot_general(
            factor_parts, jnp.concatenate([high, high, low_part], 1), CONTRACT_LAST,
            preferred_element_type=F32,
        )
        out_ref[:, pl.ds(low, width)] += float(Q) * update
    for j in range(CHUNKS):
        low, width = j * WIDTH, WIDTH
        sums = final[...] if j == 0 else finish(j)
        out_ref[:, pl.ds(low, width)] += sums * (half_cols[:, low:low + width] * -float(Q))

    for copy in sends:
        copy.wait_send()
    for i in range(3):
        y_copy(i).wait_send()
        z_copy(i).wait_send()

    @pl.when(odd == 1)
    def _():
        y_copy(3).wait_send()
        z_copy(3).wait_send()

    @pl.when(sends_panel)
    def _():
        for i in range(1, 8):
            panel_copy(i).wait_send()
        for i in range(3):
            row_copy(i).wait_send()

    @pl.when(to_another)
    def _():
        panel_copy(0).wait_send()

    assert len(used) <= N_COPIES


def shards(alignment, cluster_sizes, block_inverse):
    vmem = pl.BlockSpec(memory_space=pltpu.VMEM)

    return pl.pallas_call(
        kernel,
        out_shape=jax.ShapeDtypeStruct((ROWS, COLS), F32),
        in_specs=[pl.BlockSpec(memory_space=pl.ANY), vmem, vmem],
        out_specs=vmem,
        scratch_shapes=[
            pltpu.VMEM((SEQS_LOCAL, POS), jnp.int32),
            pltpu.VMEM((12, 8, SEQS_LOCAL), F32),
            pltpu.VMEM((10, 8, SEQS_LOCAL), F32),
            pltpu.VMEM((SEQS_LOCAL // LANES, LANES), jnp.int32),
            pltpu.VMEM((LEFT, SEQS_LOCAL), HOT),
            pltpu.VMEM((HALF, SEQS_LOCAL), HOT),
            pltpu.VMEM((COLS, SEQS_LOCAL), HOT),
            pltpu.VMEM((COLS, SEQS_LOCAL), HOT),
            pltpu.VMEM((LEFT, WIDTH), F32),
            pltpu.VMEM((7, ROWS, WIDTH), F32),
            pltpu.VMEM((CHUNKS - 1, LEFT_MERGED, WIDTH), F32),
            pltpu.VMEM((CHUNKS - 1, 6, 40, WIDTH), F32),
            pltpu.VMEM((ROWS, WIDTH), F32),
            pltpu.VMEM((16, LANES), F32),
            pltpu.VMEM((7, 16, LANES), F32),
            pltpu.VMEM((16, LANES), F32),
            pltpu.VMEM((4, 16, LANES), F32),
            pltpu.VMEM((2, 8, ROWS, PANEL), F32),
            pltpu.VMEM((ROWS, PANEL), F32),
            pltpu.VMEM((COLS, PANEL), F32),
            pltpu.SemaphoreType.DMA((SEQS_LOCAL // LOAD,)),
            pltpu.SemaphoreType.DMA((N_COPIES,)),
            pltpu.SemaphoreType.DMA((N_COPIES,)),
        ],
        compiler_params=pltpu.CompilerParams(
            collective_id=0, has_side_effects=True, vmem_limit_bytes=56 * 2**20
        ),
        name="couplings",
    )(alignment, cluster_sizes.reshape(SEQS_LOCAL // LANES, LANES), block_inverse)


def solution(mesh):
    in_specs = (P("seq", None), P("seq"), P())
    out_specs = P(("seq", "row"), "col")
    return jax.shard_map(shards, mesh=mesh, in_specs=in_specs, out_specs=out_specs, check_vma=False)
```
